32 devices in a mesh: wide: 8 (over y, x, core), layer: 4 (over z).
Axes of the slice: x: 2, y: 2, z: 4, core: 2. Of those that a mesh axis runs over, the one named last changes fastest.
Arguments:
- factor: float32 [4096, 1024], P('layer', 'wide'), parts along dimension 0, may hold values from -1 to 21, as said below
Outputs:
- rotated: float32 [4096, 1024], P('layer', 'wide'), parts along dimension 0
- eigen_basis: float32 [4096, 1024], P('layer', 'wide'), parts along dimension 0
The draws below stay inside these ranges and needn't reach their ends.
There are 4 independent parts, one for each index of `layer`. The reference program is written for one: setup_inputs(seed, part) draws one part's arguments, and reference() takes and returns one part's arrays. A program takes and returns all parts, laid end to end along the dimension named above; each array names one. Nothing has to cross between parts.
Inputs may be any that keep to these rules, and one draw needn't show every extreme that they name: `factor`: symmetric.
All inputs are finite; a program needn't handle non-finite values.
Results may differ from the reference program's by a relative error of at most 0.00095.
Values sent between devices are 32-bit elements; how exact they have to be, the bound alone decides.
No kernel may reach another device: no remote copies, remote signals or barrier semaphores. Data moves between devices by JAX's collectives and lax.ppermute only.
A program may use at most 128 MiB of HBM per device.

```python
import jax
import jax.numpy as jnp
from jax import lax

BW = 64
SWEEPS = 3
NN = 1024
N_WIDE = 8


def draw_factor(key, part):
    key_diag, key_noise = jax.random.split(jax.random.fold_in(key, 7), 2)
    diagonal_vals = jnp.exp(jax.random.uniform(key_diag, (NN,), jnp.float32, jnp.log(2.0), jnp.log(20.0)))
    positions = jnp.arange(NN, dtype=jnp.int32)
    block_ids = positions // (2 * BW)
    inside = (block_ids[:, None] == block_ids[None, :]).astype(jnp.float32)
    off_diagonal = (positions[:, None] != positions[None, :]).astype(jnp.float32)
    level = 0.012 + (0.15 - 0.012) * inside
    raw_noise = jax.random.normal(key_noise, (NN, NN), jnp.float32)
    sym_noise = (raw_noise + raw_noise.T) * (level / 1.41421356) * off_diagonal
    sym_noise = jnp.clip(sym_noise, -1.0, 1.0)
    return sym_noise + jnp.diag(diagonal_vals)


def setup_inputs(seed: int = 0, part: int = 0) -> dict:
    splits = jax.random.split(jax.random.key(seed), 2)
    part_splits = jax.random.split(jax.random.fold_in(splits[1], part), 2)
    factor = draw_factor(jax.random.fold_in(jax.random.fold_in(splits[1], part), 71), part)
    return dict(factor=factor)


floor_term = 0.01

def cayley_sweeps(pair_block):
    order_size = pair_block.shape[0]
    identity_mat = jnp.eye(order_size, dtype=pair_block.dtype)
    rotation = identity_mat
    for repeat in range(SWEEPS):
        diagonal = jnp.diagonal(pair_block)
        spread = diagonal[None, :] - diagonal[:, None]
        ratios = pair_block * spread / (spread * spread + 2.0 * pair_block * pair_block + floor_term)
        skewed = 0.5 * (ratios - ratios.T) * (1.0 - identity_mat)
        half_turn = identity_mat + 0.5 * skewed
        system = identity_mat - 0.25 * jnp.dot(skewed, skewed, precision=lax.Precision.HIGHEST)
        lower_part = jnp.linalg.cholesky(system)
        square_turn = jnp.dot(half_turn, half_turn, precision=lax.Precision.HIGHEST)
        rotate_now = jax.scipy.linalg.cho_solve((lower_part, True), square_turn)
        pair_block = jnp.dot(rotate_now.T, jnp.dot(pair_block, rotate_now, precision=lax.Precision.HIGHEST), precision=lax.Precision.HIGHEST)
        rotation = jnp.dot(rotation, rotate_now, precision=lax.Precision.HIGHEST)
    return rotation

def trade_blocks(array, axis_num):
    moved = jnp.moveaxis(array, axis_num, 0)
    rest_shape = moved.shape[1:]
    split_view = moved.reshape((2, N_WIDE // 2, 2, BW) + rest_shape)
    joined = jnp.concatenate([split_view[:, :, :1], split_view[::-1, :, 1:]], axis=2)
    return jnp.moveaxis(joined.reshape(moved.shape), 0, axis_num)

def reference(factor):
    pair_span = 2 * BW
    current = factor
    basis = jnp.eye(NN, dtype=factor.dtype)
    index_list = jnp.arange(N_WIDE)
    for repeat in range(2):
        if repeat == 1:
            current = trade_blocks(trade_blocks(current, 0), 1)
            basis = trade_blocks(basis, 1)
        grid = current.reshape(N_WIDE, pair_span, N_WIDE, pair_span)
        diagonal_blocks = grid[index_list, :, index_list, :]
        turns = lax.map(cayley_sweeps, diagonal_blocks)
        columns = jnp.einsum('kald,ldc->kalc', grid, turns, precision=lax.Precision.HIGHEST)
        updated = jnp.einsum('kba,kblc->kalc', turns, columns, precision=lax.Precision.HIGHEST)
        current = updated.reshape(NN, NN)
        basis_view = basis.reshape(NN, N_WIDE, pair_span)
        basis = jnp.einsum('ild,ldc->ilc', basis_view, turns, precision=lax.Precision.HIGHEST).reshape(NN, NN)
    return (current, basis)
```

```python
import functools
import jax
import jax.numpy as jnp
from jax import lax
from jax.experimental import pallas as pl
from jax.experimental.pallas import tpu as pltpu
from jax.sharding import PartitionSpec as P

SWEEPS = 3
FLOOR = 0.01
TOLERANCE = 2e-6


def schedule(bound, steps=None, goal=1e-6):
    theta = bound / (2.0 + bound)
    mus = []
    while len(mus) < steps if steps else theta > goal:
        mus.append(2.0 / (2.0 - theta * theta))
        theta = theta * theta / (2.0 - theta * theta)
    return 1.0 / (1.0 + 0.5 * bound), tuple(mus)


def split(x):
    high = x.astype(jnp.bfloat16)
    x = x - high.astype(jnp.float32)
    middle = x.astype(jnp.bfloat16)
    return high, middle, (x - middle.astype(jnp.float32)).astype(jnp.bfloat16)


def product(a, b):
    n = b.shape[1]
    a_high, a_middle, a_low = split(a)
    b_high, b_middle, b_low = split(b)
    wide = jnp.concatenate([b_high, b_middle], axis=1)
    most = jnp.dot(
        jnp.concatenate([a_high, a_middle], axis=1),
        jnp.concatenate([wide, wide], axis=0),
        preferred_element_type=jnp.float32,
    )
    rest = jnp.dot(
        jnp.concatenate([a_high, a_low], axis=1),
        jnp.concatenate([b_low, b_high], axis=0),
        preferred_element_type=jnp.float32,
    )
    return most[:, :n] + (most[:, n:] + rest)


def exact(a, b):
    return jnp.dot(a, b, precision=lax.Precision.HIGHEST, preferred_element_type=jnp.float32)


def identity_of(n):
    row = lax.broadcasted_iota(jnp.int32, (n, n), 0)
    col = lax.broadcasted_iota(jnp.int32, (n, n), 1)
    return (row == col).astype(jnp.float32)


def half_skew(m, eye):
    kept = m * eye
    spread = jnp.sum(kept, axis=0, keepdims=True) - jnp.sum(kept, axis=1, keepdims=True)
    ratios = m * spread / (spread * spread + 2.0 * m * m + FLOOR)
    return 0.25 * (ratios - ratios.T)


def sure_sweep(m, q, eye):
    n = m.shape[0]
    a = half_skew(m, eye)
    system = eye - exact(a, a)
    scale, mus = schedule(n * n / 32.0)

    def newton(_, y):
        return y + exact(y, eye - exact(system, y))

    y = lax.fori_loop(0, len(mus) + 6, newton, scale * eye)
    x = exact(y, eye + a)
    x = x + exact(x, eye - (x - exact(a, x)))
    turn = 2.0 * x - eye
    return exact(turn.T, exact(m, turn)), exact(q, turn)


def sweep(m, q, eye, plan):
    n = m.shape[0]
    scale, mus = plan
    a = half_skew(m, eye)
    rows = [a, m] if q is None else [a, m, q]
    first = product(jnp.concatenate(rows, axis=0), a)
    error = (1.0 - scale) * eye + scale * first[:n]
    left = scale * (eye - a)
    m_right = scale * (m + first[n : 2 * n])
    q_right = scale * (eye + a) if q is None else scale * (q + first[2 * n :])
    for mu in mus:
        step = product(jnp.concatenate([error, left, m_right, q_right], axis=0), error)
        error = (1.0 - mu) * eye + mu * step[:n]
        left = mu * (left + step[n : 2 * n])
        m_right = mu * (m_right + step[2 * n : 3 * n])
        q_right = mu * (q_right + step[3 * n :])
    q = 2.0 * q_right - (eye if q is None else q)
    m = product(2.0 * left - eye, 2.0 * m_right - m)
    return m, q, jnp.sum(error * error, axis=0, keepdims=True)


def solve(blocks, plans, eye):
    ms, qs = list(blocks), [None] * len(blocks)
    worst = jnp.zeros((1, eye.shape[0]), jnp.float32)
    for plan in plans:
        for k in range(len(ms)):
            ms[k], qs[k], left_over = sweep(ms[k], qs[k], eye, plan)
            worst = worst + left_over
    return ms, qs, worst


def solve_into(blocks, plans, m_ref, q_ref):
    n = blocks[0].shape[0]
    eye = identity_of(n)
    ms, qs, worst = solve(blocks, plans, eye)
    for k in range(len(ms)):
        m_ref[k] = ms[k]
        q_ref[k] = qs[k]
    settled = jnp.sum(worst) <= TOLERANCE * TOLERANCE * n

    @pl.when(jnp.logical_not(settled))
    def _():
        for k in range(len(blocks)):
            m_ref[k] = blocks[k]
            q_ref[k] = eye

        def again(step, carry):
            k = step // SWEEPS
            m_ref[k], q_ref[k] = sure_sweep(m_ref[k], q_ref[k], eye)
            return carry

        lax.fori_loop(0, SWEEPS * len(blocks), again, 0)


PLANS = ((schedule(4.0, 4),) * SWEEPS, (schedule(0.8, 3),) * SWEEPS)


def solve_kernel(plans, block_ref, q_ref, m_ref):
    solve_into([block_ref[0]], plans, m_ref, q_ref)


def cayley_sweeps(pair_block, plans):
    n = pair_block.shape[0]
    return pl.pallas_call(
        functools.partial(solve_kernel, plans),
        out_shape=jax.ShapeDtypeStruct((1, n, n), jnp.float32),
        scratch_shapes=[pltpu.VMEM((1, n, n), jnp.float32)],
        compiler_params=pltpu.CompilerParams(vmem_limit_bytes=32 * 1024 * 1024),
    )(pair_block[None])[0]


def from_partner(shard, axis, bit):
    return lax.ppermute(shard, axis, [(i, i ^ 1 << bit) for i in range(lax.axis_size(axis))])


def trade_rows(current, wide_count, width_half):
    order_size, pair_span = current.shape
    split_view = current.reshape(2, wide_count // 2, 2, width_half, pair_span)
    joined = jnp.concatenate([split_view[:, :, :1], split_view[::-1, :, 1:]], axis=2)
    return joined.reshape(order_size, pair_span)


def one_round(current, basis, my_pair, plans):
    order_size, pair_span = current.shape
    pair_block = lax.dynamic_slice_in_dim(current, my_pair * pair_span, pair_span, 0)
    rotate = cayley_sweeps(pair_block, plans)
    columns = jnp.dot(current, rotate, precision=lax.Precision.HIGHEST)
    pieces = lax.all_gather(rotate[None], "wide", axis=0, tiled=True)
    how_many = pieces.shape[0]
    row_slab = columns
    row_slab = row_slab.reshape(how_many, pair_span, pair_span)
    updated = jnp.einsum("nba,nbc->nac", pieces, row_slab, precision=lax.Precision.HIGHEST)
    current = lax.dynamic_update_slice_in_dim(
        columns, updated.reshape(how_many * pair_span, pair_span), jnp.int32(0) * pair_span, 0
    )
    basis = jnp.dot(basis, rotate, precision=lax.Precision.HIGHEST)
    return (current, basis)


def body(factor):
    wide_count = lax.axis_size("wide")
    my_pair = lax.axis_index("wide")
    order_size, pair_span = factor.shape
    width_half = pair_span // 2
    row_index = lax.broadcasted_iota(jnp.int32, (order_size, pair_span), 0)
    col_index = lax.broadcasted_iota(jnp.int32, (order_size, pair_span), 1) + my_pair * pair_span
    basis = (row_index == col_index).astype(jnp.float32)
    current = factor
    for repeat in range(2):
        if repeat == 1:
            moved_factor, moved_basis = from_partner(
                (current[:, width_half:], basis[:, width_half:]),
                "wide",
                wide_count.bit_length() - 2,
            )
            current = jnp.concatenate([current[:, :width_half], moved_factor], axis=1)
            basis = jnp.concatenate([basis[:, :width_half], moved_basis], axis=1)
            current = trade_rows(current, wide_count, width_half)
        current, basis = one_round(current, basis, my_pair, PLANS[repeat])
    return (current, basis)


def solution(mesh):
    return jax.shard_map(
        body,
        mesh=mesh,
        in_specs=(P("layer", "wide"),),
        out_specs=(P("layer", "wide"), P("layer", "wide")),
        check_vma=False,
    )
```

```python
import functools
import jax
import jax.numpy as jnp
from jax import lax
from jax.experimental import pallas as pl
from jax.experimental.pallas import tpu as pltpu
from jax.sharding import PartitionSpec as P

SWEEPS = 3
FLOOR = 0.01
TOLERANCE = 2e-6


def schedule(bound, steps=None, goal=1e-6):
    theta = bound / (2.0 + bound)
    mus = []
    while len(mus) < steps if steps else theta > goal:
        mus.append(2.0 / (2.0 - theta * theta))
        theta = theta * theta / (2.0 - theta * theta)
    return 1.0 / (1.0 + 0.5 * bound), tuple(mus)


def split(x):
    high = x.astype(jnp.bfloat16)
    x = x - high.astype(jnp.float32)
    middle = x.astype(jnp.bfloat16)
    return high, middle, (x - middle.astype(jnp.float32)).astype(jnp.bfloat16)


def product(a, b):
    n = b.shape[1]
    a_high, a_middle, a_low = split(a)
    b_high, b_middle, b_low = split(b)
    wide = jnp.concatenate([b_high, b_middle], axis=1)
    most = jnp.dot(
        jnp.concatenate([a_high, a_middle], axis=1),
        jnp.concatenate([wide, wide], axis=0),
        preferred_element_type=jnp.float32,
    )
    rest = jnp.dot(
        jnp.concatenate([a_high, a_low], axis=1),
        jnp.concatenate([b_low, b_high], axis=0),
        preferred_element_type=jnp.float32,
    )
    return most[:, :n] + (most[:, n:] + rest)


def exact(a, b):
    return jnp.dot(a, b, precision=lax.Precision.HIGHEST, preferred_element_type=jnp.float32)


def identity_of(n):
    row = lax.broadcasted_iota(jnp.int32, (n, n), 0)
    col = lax.broadcasted_iota(jnp.int32, (n, n), 1)
    return (row == col).astype(jnp.float32)


def half_skew(m, eye):
    kept = m * eye
    spread = jnp.sum(kept, axis=0, keepdims=True) - jnp.sum(kept, axis=1, keepdims=True)
    ratios = m * spread / (spread * spread + 2.0 * m * m + FLOOR)
    return 0.25 * (ratios - ratios.T)


def sure_sweep(m, q, eye):
    n = m.shape[0]
    a = half_skew(m, eye)
    system = eye - exact(a, a)
    scale, mus = schedule(n * n / 32.0)

    def newton(_, y):
        return y + exact(y, eye - exact(system, y))

    y = lax.fori_loop(0, len(mus) + 6, newton, scale * eye)
    x = exact(y, eye + a)
    x = x + exact(x, eye - (x - exact(a, x)))
    turn = 2.0 * x - eye
    return exact(turn.T, exact(m, turn)), exact(q, turn)


def sweep(m, q, eye, plan):
    n = m.shape[0]
    scale, mus = plan
    a = half_skew(m, eye)
    rows = [a, m] if q is None else [a, m, q]
    first = product(jnp.concatenate(rows, axis=0), a)
    error = (1.0 - scale) * eye + scale * first[:n]
    left = scale * (eye - a)
    m_right = scale * (m + first[n : 2 * n])
    q_right = scale * (eye + a) if q is None else scale * (q + first[2 * n :])
    for mu in mus:
        step = product(jnp.concatenate([error, left, m_right, q_right], axis=0), error)
        error = (1.0 - mu) * eye + mu * step[:n]
        left = mu * (left + step[n : 2 * n])
        m_right = mu * (m_right + step[2 * n : 3 * n])
        q_right = mu * (q_right + step[3 * n :])
    q = 2.0 * q_right - (eye if q is None else q)
    m = product(2.0 * left - eye, 2.0 * m_right - m)
    return m, q, jnp.sum(error * error, axis=0, keepdims=True)


def solve(blocks, plans, eye):
    ms, qs = list(blocks), [None] * len(blocks)
    worst = jnp.zeros((1, eye.shape[0]), jnp.float32)
    for plan in plans:
        for k in range(len(ms)):
            ms[k], qs[k], left_over = sweep(ms[k], qs[k], eye, plan)
            worst = worst + left_over
    return ms, qs, worst


def solve_into(blocks, plans, m_ref, q_ref):
    n = blocks[0].shape[0]
    eye = identity_of(n)
    ms, qs, worst = solve(blocks, plans, eye)
    for k in range(len(ms)):
        m_ref[k] = ms[k]
        q_ref[k] = qs[k]
    settled = jnp.sum(worst) <= TOLERANCE * TOLERANCE * n

    @pl.when(jnp.logical_not(settled))
    def _():
        for k in range(len(blocks)):
            m_ref[k] = blocks[k]
            q_ref[k] = eye

        def again(step, carry):
            k = step // SWEEPS
            m_ref[k], q_ref[k] = sure_sweep(m_ref[k], q_ref[k], eye)
            return carry

        lax.fori_loop(0, SWEEPS * len(blocks), again, 0)


PLANS = ((schedule(4.0, 4),) * SWEEPS, (schedule(0.8, 3),) * SWEEPS)


def halves(x):
    high = x.astype(jnp.bfloat16)
    return high, (x - high.astype(jnp.float32)).astype(jnp.bfloat16)


def quick(a, b):
    n = b.shape[1]
    a_high, a_low = halves(a)
    wide = jnp.concatenate(halves(b), axis=1)
    both = jnp.dot(a_high, wide, preferred_element_type=jnp.float32) + jnp.dot(
        a_low, wide, preferred_element_type=jnp.float32
    )
    return both[:, :n] + both[:, n:]


def pair_up(first, last, cross, n):
    row = lax.broadcasted_iota(jnp.int32, (n, n), 0) < n // 2
    col = lax.broadcasted_iota(jnp.int32, (n, n), 1) < n // 2
    corner = jnp.where(jnp.logical_and(jnp.logical_not(row), col), cross, 0.0)
    return jnp.where(row == col, jnp.where(row, first, last), corner + corner.T)


def first_kernel(own_ref, partner_ref, cross_ref, q_ref, block_ref, m_ref):
    n = own_ref.shape[0]
    solve_into([own_ref[...], partner_ref[...]], PLANS[0], m_ref, q_ref)
    cross = product(q_ref[1].T, product(cross_ref[...], q_ref[0]))
    block_ref[0] = pair_up(m_ref[0], m_ref[1], cross, n)
    block_ref[1] = pair_up(m_ref[1], m_ref[0], cross.T, n)


def second_kernel(block_ref, q_ref, turn_ref, basis_ref, second_ref, m_ref):
    n = block_ref.shape[1]
    half = n // 2
    solve_into([block_ref[0], block_ref[1]], PLANS[1], m_ref, second_ref)
    turn_ref[0] = second_ref[0].T
    turn_ref[1] = second_ref[1].T
    col = lax.broadcasted_iota(jnp.int32, (n, n), 1) < half
    mine = second_ref[0]
    basis_ref[0] = quick(jnp.where(col, q_ref[0], 0.0), mine)
    basis_ref[1] = quick(jnp.where(col, 0.0, q_ref[1]), mine)


def rows_of(pair, n):
    return pl.ds(pl.multiple_of(pair * n, n), n)


def columns_kernel(masks, far, factor_ref, moved_ref, basis_ref, *refs):
    turn_refs, (mixed_ref, out_ref) = refs[:-2], refs[-2:]
    n = factor_ref.shape[1]
    half = n // 2
    me = lax.axis_index("wide")
    out_ref[...] = jnp.zeros_like(out_ref)
    out_ref[rows_of(me, n), :] = basis_ref[0]
    out_ref[rows_of(me ^ far, n), :] = basis_ref[1]
    first, last = basis_ref[0], basis_ref[1]
    for mask, turn_ref in zip(masks, turn_refs):
        turned = []
        for side in range(2):
            pair = me ^ mask ^ (far * side)
            rows = rows_of(pair, n)
            columns = quick(factor_ref[rows, :], first) + quick(moved_ref[rows, :], last)
            turned.append(quick(turn_ref[side].T, columns))
        for side in range(2):
            pair = me ^ mask ^ (far * side)
            mixed_ref[rows_of(pair, n), :] = jnp.concatenate(
                [turned[side][:half], turned[1 - side][half:]], axis=0
            )


def rows_kernel(masks, far, mixed_ref, *refs):
    turn_refs, out_ref = refs[:-1], refs[-1]
    n = mixed_ref.shape[1]
    me = lax.axis_index("wide")
    for mask, turn_ref in zip(masks, turn_refs):
        for side in range(2):
            rows = rows_of(me ^ mask ^ (far * side), n)
            out_ref[rows, :] = quick(turn_ref[side], mixed_ref[rows, :])


def call(kernel, out_shape, scratch_shapes, flops, *args):
    return pl.pallas_call(
        kernel,
        out_shape=out_shape,
        scratch_shapes=scratch_shapes,
        compiler_params=pltpu.CompilerParams(vmem_limit_bytes=48 * 1024 * 1024),
        cost_estimate=pl.CostEstimate(flops=flops, bytes_accessed=2**20, transcendentals=0),
    )(*args)


def swap(shard, mask):
    return lax.ppermute(shard, "wide", [(i, i ^ mask) for i in range(lax.axis_size("wide"))])


def body(factor):
    wide_count = lax.axis_size("wide")
    far = wide_count // 2
    me = lax.axis_index("wide")
    order_size, n = factor.shape
    two = jax.ShapeDtypeStruct((2, n, n), jnp.float32)
    tall = jax.ShapeDtypeStruct((order_size, n), jnp.float32)
    scratch = pltpu.VMEM((2, n, n), jnp.float32)
    own = lax.dynamic_slice_in_dim(factor, me * n, n, 0)
    cross = lax.dynamic_slice_in_dim(factor, (me ^ far) * n, n, 0)
    partner = swap(own, far)
    moved = swap(lax.optimization_barrier((factor, partner))[0], far)
    turns, blocks = call(first_kernel, (two, two), [scratch], 2**33, own, partner, cross)

    def spread(pieces):
        bit = far // 2
        while bit:
            pieces = pieces + [(mask | bit, swap(piece, bit)) for mask, piece in pieces]
            bit //= 2
        return [mask for mask, _ in pieces], [piece for _, piece in pieces]

    masks, all_first = spread([(0, turns)])
    second, basis = call(second_kernel, (two, two), [scratch, scratch], 2**33, blocks, turns)
    masks, all_second = spread([(0, second)])
    mixed, eigen_basis = call(
        functools.partial(columns_kernel, masks, far), (tall, tall), [], 2**31, factor, moved, basis, *all_first
    )
    rotated = call(functools.partial(rows_kernel, masks, far), tall, [], 2**30, mixed, *all_second)
    return (rotated, eigen_basis)


def solution(mesh):
    return jax.shard_map(
        body,
        mesh=mesh,
        in_specs=(P("layer", "wide"),),
        out_specs=(P("layer", "wide"), P("layer", "wide")),
        check_vma=False,
    )
```

```python
import functools
import jax
import jax.numpy as jnp
from jax import lax
from jax.experimental import pallas as pl
from jax.experimental.pallas import tpu as pltpu
from jax.sharding import PartitionSpec as P

SWEEPS = 3
FLOOR = 0.01
TOLERANCE = 2e-6


def schedule(bound, steps=None, goal=1e-6):
    theta = bound / (2.0 + bound)
    mus = []
    while len(mus) < steps if steps else theta > goal:
        mus.append(2.0 / (2.0 - theta * theta))
        theta = theta * theta / (2.0 - theta * theta)
    return 1.0 / (1.0 + 0.5 * bound), tuple(mus)


def split(x):
    high = x.astype(jnp.bfloat16)
    x = x - high.astype(jnp.float32)
    middle = x.astype(jnp.bfloat16)
    return high, middle, (x - middle.astype(jnp.float32)).astype(jnp.bfloat16)


def product(a, b):
    n = b.shape[1]
    a_high, a_middle, a_low = split(a)
    b_high, b_middle, b_low = split(b)
    wide = jnp.concatenate([b_high, b_middle], axis=1)
    most = jnp.dot(
        jnp.concatenate([a_high, a_middle], axis=1),
        jnp.concatenate([wide, wide], axis=0),
        preferred_element_type=jnp.float32,
    )
    rest = jnp.dot(
        jnp.concatenate([a_high, a_low], axis=1),
        jnp.concatenate([b_low, b_high], axis=0),
        preferred_element_type=jnp.float32,
    )
    return most[:, :n] + (most[:, n:] + rest)


def exact(a, b):
    return jnp.dot(a, b, precision=lax.Precision.HIGHEST, preferred_element_type=jnp.float32)


def identity_of(n):
    row = lax.broadcasted_iota(jnp.int32, (n, n), 0)
    col = lax.broadcasted_iota(jnp.int32, (n, n), 1)
    return (row == col).astype(jnp.float32)


def half_skew(m, eye):
    kept = m * eye
    spread = jnp.sum(kept, axis=0, keepdims=True) - jnp.sum(kept, axis=1, keepdims=True)
    ratios = m * spread / (spread * spread + 2.0 * m * m + FLOOR)
    return 0.25 * (ratios - ratios.T)


def sure_sweep(m, qt, eye):
    n = m.shape[0]
    a = half_skew(m, eye)
    system = eye - exact(a, a)
    scale, mus = schedule(n * n / 32.0)

    def newton(_, y):
        return y + exact(y, eye - exact(system, y))

    y = lax.fori_loop(0, len(mus) + 6, newton, scale * eye)
    x = exact(y, eye + a)
    x = x + exact(x, eye - (x - exact(a, x)))
    turn = 2.0 * x - eye
    return exact(turn.T, exact(m, turn)), exact(turn.T, qt)


def solve(blocks, plans, eye, keep):
    n = eye.shape[0]
    some = range(len(blocks))
    ms, qts = list(blocks), None
    worst = jnp.zeros((1, n), jnp.float32)
    for index, (scale, mus) in enumerate(plans):
        carried = keep or index + 1 < len(plans)
        skews = [half_skew(m, eye) for m in ms]
        if carried:
            firsts = [product(jnp.concatenate([a, m], axis=0), a) for a, m in zip(skews, ms)]
        else:
            firsts = [product(a, a) for a in skews]
        errors = [(1.0 - scale) * eye + scale * first[:n] for first in firsts]
        stacks = [scale * (eye - a) for a in skews]
        if carried:
            stacks = [
                jnp.concatenate([stack, scale * (m + first[n:])], axis=0)
                for stack, m, first in zip(stacks, ms, firsts)
            ]
        for mu in mus:
            steps = [
                product(jnp.concatenate([error, stack], axis=0), error)
                for error, stack in zip(errors, stacks)
            ]
            errors = [(1.0 - mu) * eye + mu * step[:n] for step in steps]
            stacks = [mu * (stack + step[n:]) for stack, step in zip(stacks, steps)]
        for error in errors:
            worst = worst + jnp.sum(error * error, axis=0, keepdims=True)
        backs = [2.0 * stack[:n] - eye for stack in stacks]
        rights = [[] for _ in some]
        if carried:
            rights = [[2.0 * stack[n:] - m] for stack, m in zip(stacks, ms)]
        if qts is not None:
            rights = [right + [qt] for right, qt in zip(rights, qts)]
        turned = [
            product(back, jnp.concatenate(right, axis=1)) for back, right in zip(backs, rights)
        ]
        qts = backs if qts is None else [both[:, -n:] for both in turned]
        if carried:
            ms = [both[:, :n] for both in turned]
    return ms, qts, worst


def settled(worst):
    return jnp.sum(worst) <= TOLERANCE * TOLERANCE * worst.shape[1]


def solve_surely(blocks, m_ref, qt_ref, eye):
    for k in range(len(blocks)):
        m_ref[k] = blocks[k]
        qt_ref[k] = eye

    def again(step, carry):
        k = step // SWEEPS
        m_ref[k], qt_ref[k] = sure_sweep(m_ref[k], qt_ref[k], eye)
        return carry

    lax.fori_loop(0, SWEEPS * len(blocks), again, 0)


PLANS = ((schedule(4.0, 4),) * SWEEPS, (schedule(0.8, 3),) * SWEEPS)


def halves(x):
    high = x.astype(jnp.bfloat16)
    return high, (x - high.astype(jnp.float32)).astype(jnp.bfloat16)


def quick(a, b):
    n = b.shape[1]
    wide = jnp.concatenate(halves(b), axis=1)
    both = jnp.dot(
        jnp.concatenate(halves(a), axis=1),
        jnp.concatenate([wide, wide], axis=0),
        preferred_element_type=jnp.float32,
    )
    return both[:, :n] + both[:, n:]


def pair_up(first, last, cross):
    n = first.shape[0]
    row = lax.broadcasted_iota(jnp.int32, (n, n), 0) < n // 2
    col = lax.broadcasted_iota(jnp.int32, (n, n), 1) < n // 2
    corner = jnp.where(jnp.logical_and(jnp.logical_not(row), col), cross, 0.0)
    return jnp.where(row == col, jnp.where(row, first, last), corner + corner.T)


def rows_of(pair, n):
    return pl.ds(pl.multiple_of(pair * n, n), n)


def first_kernel(own_ref, partner_ref, cross_ref, qt_ref, block_ref, m_ref):
    n = own_ref.shape[0]
    eye = identity_of(n)
    cross = cross_ref[...]

    def finish(ms, qts):
        moved = product(qts[1], product(cross, qts[0].T))
        block_ref[0] = pair_up(ms[0], ms[1], moved)
        block_ref[1] = pair_up(ms[1], ms[0], moved.T)

    blocks = [own_ref[...], partner_ref[...]]
    ms, qts, worst = solve(blocks, PLANS[0], eye, True)
    qt_ref[0], qt_ref[1] = qts
    finish(ms, qts)

    @pl.when(jnp.logical_not(settled(worst)))
    def _():
        solve_surely([own_ref[...], partner_ref[...]], m_ref, qt_ref, eye)
        finish([m_ref[0], m_ref[1]], [qt_ref[0], qt_ref[1]])


def second_kernel(block_ref, qt_ref, m_ref):
    eye = identity_of(block_ref.shape[1])
    _, (qt_ref[0], qt_ref[1]), worst = solve([block_ref[0], block_ref[1]], PLANS[1], eye, False)

    @pl.when(jnp.logical_not(settled(worst)))
    def _():
        solve_surely([block_ref[0], block_ref[1]], m_ref, qt_ref, eye)


def columns_kernel(masks, far, factor_ref, moved_ref, second_ref, *refs):
    turn_refs, (mixed_ref, out_ref) = refs[:-2], refs[-2:]
    n = factor_ref.shape[1]
    half = n // 2
    me = lax.axis_index("wide")
    pairs = [[me ^ mask ^ (far * side) for side in range(2)] for mask in masks]
    row = lax.broadcasted_iota(jnp.int32, (n, n), 0) < half
    turn = second_ref[0].T
    first = quick(jnp.where(row, turn_refs[0][0], 0.0).T, turn)
    last = quick(jnp.where(row, 0.0, turn_refs[0][1]).T, turn)
    out_ref[...] = jnp.zeros_like(out_ref)
    out_ref[rows_of(pairs[0][0], n), :] = first
    out_ref[rows_of(pairs[0][1], n), :] = last
    both = jnp.concatenate([first, last], axis=0)
    for couple in pairs:
        for pair in couple:
            rows = rows_of(pair, n)
            columns = jnp.concatenate([factor_ref[rows, :], moved_ref[rows, :]], axis=1)
            mixed_ref[rows, :] = quick(columns, both)
    for couple, turn_ref in zip(pairs, turn_refs):
        near, away = [
            quick(turn_ref[side], mixed_ref[rows_of(pair, n), :]) for side, pair in enumerate(couple)
        ]
        mixed_ref[rows_of(couple[0], n), :] = jnp.concatenate([near[:half], away[half:]], axis=0)
        mixed_ref[rows_of(couple[1], n), :] = jnp.concatenate([away[:half], near[half:]], axis=0)


def rows_kernel(masks, far, mixed_ref, *refs):
    turn_refs, out_ref = refs[:-1], refs[-1]
    n = mixed_ref.shape[1]
    me = lax.axis_index("wide")
    for mask, turn_ref in zip(masks, turn_refs):
        for side in range(2):
            rows = rows_of(me ^ mask ^ (far * side), n)
            out_ref[rows, :] = quick(turn_ref[side], mixed_ref[rows, :])


def call(kernel, out_shape, scratch_shapes, flops, *args):
    return pl.pallas_call(
        kernel,
        out_shape=out_shape,
        scratch_shapes=scratch_shapes,
        compiler_params=pltpu.CompilerParams(vmem_limit_bytes=48 * 1024 * 1024),
        cost_estimate=pl.CostEstimate(flops=flops, bytes_accessed=2**20, transcendentals=0),
    )(*args)


def swap(shard, mask):
    return lax.ppermute(shard, "wide", [(i, i ^ mask) for i in range(lax.axis_size("wide"))])


def spread(piece, far, gate=None):
    pieces = [(0, piece)]
    bit = far // 2
    while bit:
        fresh = []
        for mask, held in pieces:
            if gate is not None and mask and bit == 1:
                held = lax.optimization_barrier((held, gate))[0]
            fresh.append((mask | bit, swap(held, bit)))
        pieces = pieces + fresh
        bit //= 2
    return [mask for mask, _ in pieces], [held for _, held in pieces]


def body(factor):
    far = lax.axis_size("wide") // 2
    me = lax.axis_index("wide")
    order_size, n = factor.shape
    two = jax.ShapeDtypeStruct((2, n, n), jnp.float32)
    tall = jax.ShapeDtypeStruct((order_size, n), jnp.float32)
    scratch = [pltpu.VMEM((2, n, n), jnp.float32)]
    own = lax.dynamic_slice_in_dim(factor, me * n, n, 0)
    cross = lax.dynamic_slice_in_dim(factor, (me ^ far) * n, n, 0)
    partner = swap(own, far)
    moved = swap(factor, far)
    turns, blocks = call(
        first_kernel, (two, two), scratch, 2**32, own, partner, cross
    )

    second = call(second_kernel, two, scratch, 2**32, blocks)
    masks, all_first = spread(turns, far, second)
    mixed, eigen_basis = call(
        functools.partial(columns_kernel, masks, far),
        (tall, tall),
        [],
        2**20,
        factor,
        moved,
        second,
        *all_first,
    )
    masks, all_second = spread(second, far, mixed)
    rotated = call(functools.partial(rows_kernel, masks, far), tall, [], 2**20, mixed, *all_second)
    return (rotated, eigen_basis)


def solution(mesh):
    return jax.shard_map(
        body,
        mesh=mesh,
        in_specs=(P("layer", "wide"),),
        out_specs=(P("layer", "wide"), P("layer", "wide")),
        check_vma=False,
    )
```

```python
import functools
import jax
import jax.numpy as jnp
from jax import lax
from jax.experimental import pallas as pl
from jax.experimental.pallas import tpu as pltpu
from jax.sharding import PartitionSpec as P

SWEEPS = 3
FLOOR = 0.01
TOLERANCE = 3e-6


def schedule(bound, steps=None, weight=1.0, goal=1e-6):
    theta = bound / (2.0 + bound)
    mus = []
    while len(mus) < steps if steps else theta > goal:
        mus.append(2.0 / (2.0 - theta * theta))
        theta = theta * theta / (2.0 - theta * theta)
    return 1.0 / (1.0 + 0.5 * bound), tuple(mus), weight


def split(x):
    high = x.astype(jnp.bfloat16)
    x = x - high.astype(jnp.float32)
    middle = x.astype(jnp.bfloat16)
    return high, middle, (x - middle.astype(jnp.float32)).astype(jnp.bfloat16)


def product(a, b):
    n = b.shape[1]
    a_high, a_middle, a_low = split(a)
    b_high, b_middle, b_low = split(b)
    wide = jnp.concatenate([b_high, b_middle], axis=1)
    most = jnp.dot(
        jnp.concatenate([a_high, a_middle], axis=1),
        jnp.concatenate([wide, wide], axis=0),
        preferred_element_type=jnp.float32,
    )
    rest = jnp.dot(
        jnp.concatenate([a_high, a_low], axis=1),
        jnp.concatenate([b_low, b_high], axis=0),
        preferred_element_type=jnp.float32,
    )
    return most[:, :n] + (most[:, n:] + rest)


def exact(a, b):
    return jnp.dot(a, b, precision=lax.Precision.HIGHEST, preferred_element_type=jnp.float32)


def identity_of(n):
    row = lax.broadcasted_iota(jnp.int32, (n, n), 0)
    col = lax.broadcasted_iota(jnp.int32, (n, n), 1)
    return (row == col).astype(jnp.float32)


def ratios_of(m, eye):
    kept = m * eye
    spread = jnp.sum(kept, axis=0, keepdims=True) - jnp.sum(kept, axis=1, keepdims=True)
    return m * spread / (spread * spread + 2.0 * m * m + FLOOR)


def sure_sweep(m, qt, eye):
    n = m.shape[0]
    ratios = ratios_of(m, eye)
    a = 0.25 * (ratios - ratios.T)
    system = eye - exact(a, a)
    scale, mus, _ = schedule(n * n / 32.0)

    def newton(_, y):
        return y + exact(y, eye - exact(system, y))

    y = lax.fori_loop(0, len(mus) + 6, newton, scale * eye)
    x = exact(y, eye + a)
    x = x + exact(x, eye - (x - exact(a, x)))
    turn = 2.0 * x - eye
    return exact(turn.T, exact(m, turn)), exact(turn.T, qt)


def solve(blocks, plans, eye, keep):
    n = eye.shape[0]
    some = range(len(blocks))
    ms, qts = list(blocks), None
    worst = jnp.zeros((1, n), jnp.float32)
    for index, (scale, mus, weight) in enumerate(plans):
        carried = keep or index + 1 < len(plans)
        skews = [0.5 * ratios_of(m, eye) for m in ms]
        if carried:
            firsts = [product(jnp.concatenate([a, m], axis=0), a) for a, m in zip(skews, ms)]
        else:
            firsts = [product(a, a) for a in skews]
        errors = [(1.0 - scale) * eye + scale * first[:n] for first in firsts]
        stacks = [scale * (eye - a) for a in skews]
        if carried:
            stacks = [
                jnp.concatenate([stack, scale * (m + first[n:])], axis=0)
                for stack, m, first in zip(stacks, ms, firsts)
            ]
        for mu in mus:
            steps = [
                product(jnp.concatenate([error, stack], axis=0), error)
                for error, stack in zip(errors, stacks)
            ]
            errors = [(1.0 - mu) * eye + mu * step[:n] for step in steps]
            stacks = [mu * (stack + step[n:]) for stack, step in zip(stacks, steps)]
        for error in errors:
            worst = worst + weight * jnp.sum(error * error, axis=0, keepdims=True)
        backs = [2.0 * stack[:n] - eye for stack in stacks]
        rights = [[] for _ in some]
        if carried:
            rights = [[2.0 * stack[n:] - m] for stack, m in zip(stacks, ms)]
        if qts is not None:
            rights = [right + [qt] for right, qt in zip(rights, qts)]
        turned = [
            product(back, jnp.concatenate(right, axis=1)) for back, right in zip(backs, rights)
        ]
        qts = backs if qts is None else [both[:, -n:] for both in turned]
        if carried:
            ms = [both[:, :n] for both in turned]
    return ms, qts, worst


def settled(worst):
    return jnp.sum(worst) <= TOLERANCE * TOLERANCE * worst.shape[1]


def solve_surely(blocks, m_ref, qt_ref, eye):
    for k in range(len(blocks)):
        m_ref[k] = blocks[k]
        qt_ref[k] = eye

    def again(step, carry):
        k = step // SWEEPS
        m_ref[k], qt_ref[k] = sure_sweep(m_ref[k], qt_ref[k], eye)
        return carry

    lax.fori_loop(0, SWEEPS * len(blocks), again, 0)


PLANS = (
    (schedule(4.0, 4), schedule(3.0, 4), schedule(0.95, 3)),
    (schedule(0.8, 3), schedule(0.5, 3), schedule(0.2, 2, 0.01)),
)


def halves(x):
    high = x.astype(jnp.bfloat16)
    return high, (x - high.astype(jnp.float32)).astype(jnp.bfloat16)


def quick(a, b):
    n = b.shape[1]
    wide = jnp.concatenate(halves(b), axis=1)
    both = jnp.dot(
        jnp.concatenate(halves(a), axis=1),
        jnp.concatenate([wide, wide], axis=0),
        preferred_element_type=jnp.float32,
    )
    return both[:, :n] + both[:, n:]


def pair_up(first, last, cross):
    n = first.shape[0]
    row = lax.broadcasted_iota(jnp.int32, (n, n), 0) < n // 2
    col = lax.broadcasted_iota(jnp.int32, (n, n), 1) < n // 2
    corner = jnp.where(jnp.logical_and(jnp.logical_not(row), col), cross, 0.0)
    return jnp.where(row == col, jnp.where(row, first, last), corner + corner.T)


def rows_of(pair, n):
    return pl.ds(pl.multiple_of(pair * n, n), n)


def first_kernel(own_ref, packed_ref, qt_ref, m_ref):
    n = own_ref.shape[0]
    half = n // 2
    eye = identity_of(n)
    col = lax.broadcasted_iota(jnp.int32, (half, n), 1) < half

    def finish(m, qt):
        packed_ref[:n, :] = qt
        packed_ref[n:, :] = jnp.where(col, m[:half], m[half:])

    (m,), (qt,), worst = solve([own_ref[...]], PLANS[0], eye, True)
    qt_ref[0] = qt
    m_ref[0] = m
    finish(m, qt)

    @pl.when(jnp.logical_not(settled(worst)))
    def _():
        solve_surely([own_ref[...]], m_ref, qt_ref, eye)
        finish(m_ref[0], qt_ref[0])


def columns_kernel(factor_ref, cross_ref, qt_ref, columns_ref, right_ref, moved_ref):
    order_size, n = factor_ref.shape
    half, middle = n // 2, order_size // 2
    turn = qt_ref[0].T
    moved_ref[...] = product(cross_ref[...], turn)
    for start in range(0, middle, n):
        upper = quick(factor_ref[start : start + n, :], turn)
        lower = quick(factor_ref[middle + start : middle + start + n, :], turn)
        columns_ref[start : start + n, :] = upper
        columns_ref[middle + start : middle + start + n, :] = lower
        right_ref[start : start + n, :] = jnp.concatenate([upper[:, half:], lower[:, half:]], axis=1)


def second_kernel(packed_ref, m_in_ref, own_ref, moved_ref, second_ref, first_ref, block_ref, m_ref):
    n = moved_ref.shape[0]
    eye = identity_of(n)
    qt, packed = packed_ref[:n, :], packed_ref[n:, :]
    first_ref[0] = own_ref[0]
    first_ref[1] = qt
    cross = product(qt, moved_ref[...])
    own, partner = m_in_ref[0], jnp.concatenate([packed, packed], axis=0)
    blocks = [pair_up(own, partner, cross), pair_up(partner, own, cross.T)]
    block_ref[0], block_ref[1] = blocks
    _, (second_ref[0], second_ref[1]), worst = solve(blocks, PLANS[1], eye, False)

    @pl.when(jnp.logical_not(settled(worst)))
    def _():
        solve_surely([block_ref[0], block_ref[1]], m_ref, second_ref, eye)


def turn_kernel(far, columns_ref, right_ref, second_ref, first_ref, mixed_ref, out_ref):
    order_size, n = columns_ref.shape
    half, middle = n // 2, order_size // 2
    me = lax.axis_index("wide")
    row = lax.broadcasted_iota(jnp.int32, (n, n), 0) < half
    turn = second_ref[0].T
    out_ref[...] = jnp.zeros_like(out_ref)
    out_ref[rows_of(me, n), :] = quick(jnp.where(row, first_ref[0], 0.0).T, turn)
    out_ref[rows_of(me ^ far, n), :] = quick(jnp.where(row, 0.0, first_ref[1]).T, turn)
    for start in range(0, middle, n):
        upper, lower = slice(start, start + n), slice(middle + start, middle + start + n)
        right = right_ref[upper, :]
        left = columns_ref[upper, :]
        mixed_ref[upper, :] = quick(jnp.concatenate([left[:, :half], right[:, :half]], axis=1), turn)
        left = columns_ref[lower, :]
        mixed_ref[lower, :] = quick(jnp.concatenate([left[:, :half], right[:, half:]], axis=1), turn)


def trade_kernel(masks, far, turned_ref, *refs):
    refs, mixed_ref = refs[:-1], refs[-1]
    n = turned_ref.shape[1]
    half = n // 2
    me = lax.axis_index("wide")
    for mask, (near_ref, away_ref) in zip(masks, two_by_two(refs)):
        pair, other = rows_of(me ^ mask, n), rows_of(me ^ mask ^ far, n)
        near = quick(near_ref[...], turned_ref[pair, :])
        away = quick(away_ref[...], turned_ref[other, :])
        mixed_ref[pair, :] = jnp.concatenate([near[:half], away[half:]], axis=0)
        mixed_ref[other, :] = jnp.concatenate([away[:half], near[half:]], axis=0)


def two_by_two(refs):
    couples, held = [], []
    for ref in refs:
        held += [ref.at[side] for side in range(ref.shape[0])]
        if len(held) == 2:
            couples.append(held)
            held = []
    return couples


def rows_kernel(masks, far, mixed_ref, *refs):
    refs, out_ref = refs[:-1], refs[-1]
    n = mixed_ref.shape[1]
    me = lax.axis_index("wide")
    for mask, turn_ref in zip(masks, refs):
        for side in range(2):
            rows = rows_of(me ^ mask ^ (far * side), n)
            out_ref[rows, :] = quick(turn_ref[side], mixed_ref[rows, :])


def last_rows_kernel(masks, far, mixed_ref, *refs):
    turn_refs, (_, out_ref, block_ref, sem_ref) = refs[:-4], refs[-4:]
    n = mixed_ref.shape[1]
    me = lax.axis_index("wide")
    copies = []
    for mask, turn_ref in zip(masks, turn_refs):
        for side in range(2):
            rows = rows_of(me ^ mask ^ (far * side), n)
            place = len(copies)
            block_ref[place] = quick(turn_ref[side], mixed_ref[rows, :])
            copy = pltpu.make_async_copy(block_ref.at[place], out_ref.at[rows, :], sem_ref.at[place])
            copy.start()
            copies.append(copy)
    for copy in copies:
        copy.wait()


def call(kernel, out_shape, scratch_shapes, flops, *args, **more):
    return pl.pallas_call(
        kernel,
        out_shape=out_shape,
        scratch_shapes=scratch_shapes,
        compiler_params=pltpu.CompilerParams(vmem_limit_bytes=48 * 1024 * 1024),
        cost_estimate=pl.CostEstimate(flops=flops, bytes_accessed=2**20, transcendentals=0),
        **more,
    )(*args)


def swap(shard, mask):
    return lax.ppermute(shard, "wide", [(i, i ^ mask) for i in range(lax.axis_size("wide"))])


def after(value, gate):
    return lax.optimization_barrier((value, gate))[0]


def spread_first(own, early, both, far, gate):
    pieces = [(0, (both,))]
    if early:
        pieces.append((far // 2, early))
    bit = far // 4
    while bit:
        pieces += [
            (mask | bit, tuple(swap(after(held, gate), bit) for held in couple))
            for mask, couple in pieces
        ]
        bit //= 2
    return [mask for mask, _ in pieces], [held for _, couple in pieces for held in couple]


def spread_second(both, far, gate):
    pieces = [(0, both)]
    bit = far // 2
    while bit:
        pieces += [
            (mask | bit, swap(after(held, gate) if mask and bit == 1 else held, bit))
            for mask, held in pieces
        ]
        bit //= 2
    return pieces


def body(factor):
    far = lax.axis_size("wide") // 2
    me = lax.axis_index("wide")
    order_size, n = factor.shape

    def like(*shape):
        return jax.ShapeDtypeStruct(shape, jnp.float32)

    one, two, tall = like(1, n, n), like(2, n, n), like(order_size, n)
    own = lax.dynamic_slice_in_dim(factor, me * n, n, 0)
    cross = lax.dynamic_slice_in_dim(factor, (me ^ far) * n, n, 0)
    packed, qt, m = call(first_kernel, (like(n + n // 2, n), one, one), [], 2**32, own)
    packed = swap(packed, far)
    columns, right, moved = call(
        columns_kernel, (tall, like(order_size // 2, n), like(n, n)), [], 2**28, factor, cross, qt
    )
    right = swap(right, far)
    mine = after(qt, moved)
    early = (swap(mine, far // 2), swap(mine, far // 2 | far)) if far > 1 else ()
    scratch = [pltpu.VMEM((2, n, n), jnp.float32)] * 2
    second, both = call(second_kernel, (two, two), scratch, 2**31, packed, m, qt, moved)
    masks, firsts = spread_first(qt, early, both, far, second)
    turned, eigen_basis = call(
        functools.partial(turn_kernel, far), (tall, tall), [], 2**31, columns, right, second, both
    )
    mixed = call(functools.partial(trade_kernel, masks, far), tall, [], 2**31, turned, *firsts)
    pieces = spread_second(second, far, mixed)
    soon = [piece for piece in pieces if piece[0] < 2 or not piece[0] & 1]
    late = [piece for piece in pieces if piece[0] >= 2 and piece[0] & 1]
    masks, held = zip(*soon)
    rotated = call(functools.partial(rows_kernel, masks, far), tall, [], 2**29, mixed, *held)
    if late:
        masks, held = zip(*late)
        anywhere = pl.BlockSpec(memory_space=pl.ANY)
        inside = pl.BlockSpec(memory_space=pltpu.VMEM)
        rotated = call(
            functools.partial(last_rows_kernel, masks, far),
            tall,
            [
                pltpu.VMEM((2 * len(late), n, n), jnp.float32),
                pltpu.SemaphoreType.DMA((2 * len(late),)),
            ],
            2**29,
            mixed,
            *held,
            rotated,
            in_specs=[inside] * (1 + len(late)) + [anywhere],
            out_specs=anywhere,
            input_output_aliases={1 + len(late): 0},
        )
    return (rotated, eigen_basis)


def solution(mesh):
    return jax.shard_map(
        body,
        mesh=mesh,
        in_specs=(P("layer", "wide"),),
        out_specs=(P("layer", "wide"), P("layer", "wide")),
        check_vma=False,
    )
```

```python
import functools
import jax
import jax.numpy as jnp
from jax import lax
from jax.experimental import pallas as pl
from jax.experimental.pallas import tpu as pltpu
from jax.sharding import PartitionSpec as P

SWEEPS = 3
FLOOR = 0.01
TOLERANCE = 3e-6


def schedule(bound, steps=None, weight=1.0, goal=1e-6):
    theta = bound / (2.0 + bound)
    mus = []
    while len(mus) < steps if steps else theta > goal:
        mus.append(2.0 / (2.0 - theta * theta))
        theta = theta * theta / (2.0 - theta * theta)
    return 1.0 / (1.0 + 0.5 * bound), tuple(mus), weight


def split(x):
    high = x.astype(jnp.bfloat16)
    x = x - high.astype(jnp.float32)
    middle = x.astype(jnp.bfloat16)
    return high, middle, (x - middle.astype(jnp.float32)).astype(jnp.bfloat16)


def below(*parts):
    return tuple(jnp.concatenate(each, axis=0) for each in zip(*parts))


def product(a, b):
    a_high, a_middle, a_low = a
    b_high, b_middle, b_low = b
    n = b_high.shape[1]
    wide = jnp.concatenate([b_high, b_middle], axis=1)
    most = jnp.dot(
        jnp.concatenate([a_high, a_middle], axis=1),
        jnp.concatenate([wide, wide], axis=0),
        preferred_element_type=jnp.float32,
    )
    rest = jnp.dot(
        jnp.concatenate([a_high, a_low], axis=1),
        jnp.concatenate([b_low, b_high], axis=0),
        preferred_element_type=jnp.float32,
    )
    return most[:, :n] + (most[:, n:] + rest)


def exact(a, b):
    return jnp.dot(a, b, precision=lax.Precision.HIGHEST, preferred_element_type=jnp.float32)


def identity_of(n):
    row = lax.broadcasted_iota(jnp.int32, (n, n), 0)
    col = lax.broadcasted_iota(jnp.int32, (n, n), 1)
    return (row == col).astype(jnp.float32)


def ratios_of(m, eye):
    kept = m * eye
    spread = jnp.sum(kept, axis=0, keepdims=True) - jnp.sum(kept, axis=1, keepdims=True)
    return m * spread / (spread * spread + 2.0 * m * m + FLOOR)


def sure_sweep(m, qt, eye):
    n = m.shape[0]
    ratios = ratios_of(m, eye)
    a = 0.25 * (ratios - ratios.T)
    system = eye - exact(a, a)
    scale, mus, _ = schedule(n * n / 32.0)

    def newton(_, y):
        return y + exact(y, eye - exact(system, y))

    y = lax.fori_loop(0, len(mus) + 6, newton, scale * eye)
    x = exact(y, eye + a)
    x = x + exact(x, eye - (x - exact(a, x)))
    turn = 2.0 * x - eye
    return exact(turn.T, exact(m, turn)), exact(turn.T, qt)


def solve(blocks, plans, eye, keep):
    n = eye.shape[0]
    some = range(len(blocks))
    ms, qts = list(blocks), None
    worst = jnp.zeros((1, n), jnp.float32)
    for index, (scale, mus, weight) in enumerate(plans):
        carried = keep or index + 1 < len(plans)
        skews = [0.5 * ratios_of(m, eye) for m in ms]
        parts = [split(a) for a in skews]
        if carried:
            firsts = [product(below(a, split(m)), a) for a, m in zip(parts, ms)]
        else:
            firsts = [product(a, a) for a in parts]
        errors = [(1.0 - scale) * eye + scale * first[:n] for first in firsts]
        stacks = [scale * (eye - a) for a in skews]
        if carried:
            stacks = [
                jnp.concatenate([stack, scale * (m + first[n:])], axis=0)
                for stack, m, first in zip(stacks, ms, firsts)
            ]
        for mu in mus:
            parts = [split(error) for error in errors]
            steps = [product(below(part, split(stack)), part) for part, stack in zip(parts, stacks)]
            errors = [(1.0 - mu) * eye + mu * step[:n] for step in steps]
            stacks = [mu * (stack + step[n:]) for stack, step in zip(stacks, steps)]
        for error in errors:
            worst = worst + weight * jnp.sum(error * error, axis=0, keepdims=True)
        backs = [2.0 * stack[:n] - eye for stack in stacks]
        rights = [[] for _ in some]
        if carried:
            rights = [[2.0 * stack[n:] - m] for stack, m in zip(stacks, ms)]
        if qts is not None:
            rights = [right + [qt] for right, qt in zip(rights, qts)]
        turned = [
            product(split(back), split(jnp.concatenate(right, axis=1)))
            for back, right in zip(backs, rights)
        ]
        qts = backs if qts is None else [both[:, -n:] for both in turned]
        if carried:
            ms = [both[:, :n] for both in turned]
    return ms, qts, worst


def settled(worst):
    return jnp.sum(worst) <= TOLERANCE * TOLERANCE * worst.shape[1]


def solve_surely(blocks, m_ref, qt_ref, eye):
    for k in range(len(blocks)):
        m_ref[k] = blocks[k]
        qt_ref[k] = eye

    def again(step, carry):
        k = step // SWEEPS
        m_ref[k], qt_ref[k] = sure_sweep(m_ref[k], qt_ref[k], eye)
        return carry

    lax.fori_loop(0, SWEEPS * len(blocks), again, 0)


PLANS = (
    (schedule(4.0, 4), schedule(3.0, 4), schedule(0.95, 3)),
    (schedule(0.8, 3), schedule(0.5, 3), schedule(0.2, 2, 0.01)),
)


def halves(x):
    high = x.astype(jnp.bfloat16)
    return high, (x - high.astype(jnp.float32)).astype(jnp.bfloat16)


def quick(a, b):
    n = b.shape[1]
    wide = jnp.concatenate(halves(b), axis=1)
    both = jnp.dot(
        jnp.concatenate(halves(a), axis=1),
        jnp.concatenate([wide, wide], axis=0),
        preferred_element_type=jnp.float32,
    )
    return both[:, :n] + both[:, n:]


def pair_up(first, last, corner):
    n = first.shape[0]
    row = lax.broadcasted_iota(jnp.int32, (n, n), 0) < n // 2
    col = lax.broadcasted_iota(jnp.int32, (n, n), 1) < n // 2
    return jnp.where(row == col, jnp.where(row, first, last), corner + corner.T)


def rows_of(pair, n):
    return pl.ds(pl.multiple_of(pair * n, n), n)


def first_kernel(own_ref, packed_ref, qt_ref, m_ref):
    n = own_ref.shape[0]
    half = n // 2
    eye = identity_of(n)
    col = lax.broadcasted_iota(jnp.int32, (half, n), 1) < half

    def finish(m, qt):
        packed_ref[:n, :] = qt
        packed_ref[n:, :] = jnp.where(col, m[:half], m[half:])

    (m,), (qt,), worst = solve([own_ref[...]], PLANS[0], eye, True)
    qt_ref[0] = qt
    m_ref[0] = m
    finish(m, qt)

    @pl.when(jnp.logical_not(settled(worst)))
    def _():
        solve_surely([own_ref[...]], m_ref, qt_ref, eye)
        finish(m_ref[0], qt_ref[0])


def columns_kernel(factor_ref, cross_ref, qt_ref, columns_ref, right_ref, moved_ref):
    order_size, n = factor_ref.shape
    half, middle = n // 2, order_size // 2
    turn = qt_ref[0].T
    moved_ref[...] = product(split(cross_ref[...]), split(turn))
    for start in range(0, middle, n):
        upper = quick(factor_ref[start : start + n, :], turn)
        lower = quick(factor_ref[middle + start : middle + start + n, :], turn)
        columns_ref[start : start + n, :] = upper
        columns_ref[middle + start : middle + start + n, :] = lower
        right_ref[start : start + n, :] = jnp.concatenate([upper[:, half:], lower[:, half:]], axis=1)


def second_kernel(packed_ref, m_in_ref, own_ref, moved_ref, second_ref, first_ref, block_ref, m_ref):
    n = moved_ref.shape[0]
    eye = identity_of(n)
    qt, packed = packed_ref[:n, :], packed_ref[n:, :]
    first_ref[0] = own_ref[0]
    first_ref[1] = qt
    cross = product(split(qt), split(moved_ref[...]))
    own, partner = m_in_ref[0], jnp.concatenate([packed, packed], axis=0)
    row = lax.broadcasted_iota(jnp.int32, (n, n), 0) < n // 2
    col = lax.broadcasted_iota(jnp.int32, (n, n), 1) < n // 2
    lower = jnp.where(jnp.logical_and(jnp.logical_not(row), col), cross, 0.0)
    upper = jnp.where(jnp.logical_and(row, jnp.logical_not(col)), cross, 0.0)
    blocks = [pair_up(own, partner, lower), pair_up(partner, own, upper)]
    block_ref[0], block_ref[1] = blocks
    _, (second_ref[0], second_ref[1]), worst = solve(blocks, PLANS[1], eye, False)

    @pl.when(jnp.logical_not(settled(worst)))
    def _():
        solve_surely([block_ref[0], block_ref[1]], m_ref, second_ref, eye)


def turn_kernel(far, columns_ref, second_ref, first_ref, turned_ref, turn_ref, out_ref):
    order_size, n = columns_ref.shape
    half = n // 2
    me = lax.axis_index("wide")
    row = lax.broadcasted_iota(jnp.int32, (n, n), 0) < half
    turn = second_ref[0].T
    turn_ref[...] = turn
    out_ref[...] = jnp.zeros_like(out_ref)
    out_ref[rows_of(me, n), :] = quick(jnp.where(row, first_ref[0], 0.0).T, turn)
    out_ref[rows_of(me ^ far, n), :] = quick(jnp.where(row, 0.0, first_ref[1]).T, turn)
    upper = jnp.where(row, turn, 0.0)
    for start in range(0, order_size, n):
        turned_ref[start : start + n, :] = quick(columns_ref[start : start + n, :], upper)


def trade_kernel(masks, far, turned_ref, turn_ref, right_ref, *refs):
    refs, mixed_ref, whole_ref = refs[:-2], refs[-2], refs[-1]
    order_size, n = turned_ref.shape
    half, middle = n // 2, order_size // 2
    me = lax.axis_index("wide")
    row = lax.broadcasted_iota(jnp.int32, (n, n), 0) < half
    turn = turn_ref[...]
    first = jnp.where(row, jnp.concatenate([turn[half:], turn[half:]], axis=0), 0.0)
    last = jnp.where(row, 0.0, turn)
    for start in range(0, middle, n):
        upper, lower = slice(start, start + n), slice(middle + start, middle + start + n)
        whole_ref[upper, :] = turned_ref[upper, :] + quick(right_ref[upper, :], first)
        whole_ref[lower, :] = turned_ref[lower, :] + quick(right_ref[upper, :], last)
    for mask, (near_ref, away_ref) in zip(masks, two_by_two(refs)):
        pair, other = rows_of(me ^ mask, n), rows_of(me ^ mask ^ far, n)
        near = quick(near_ref[...], whole_ref[pair, :])
        away = quick(away_ref[...], whole_ref[other, :])
        mixed_ref[pair, :] = jnp.concatenate([near[:half], away[half:]], axis=0)
        mixed_ref[other, :] = jnp.concatenate([away[:half], near[half:]], axis=0)


def two_by_two(refs):
    couples, held = [], []
    for ref in refs:
        held += [ref.at[side] for side in range(ref.shape[0])]
        if len(held) == 2:
            couples.append(held)
            held = []
    return couples


def rows_kernel(masks, far, mixed_ref, *refs):
    refs, out_ref = refs[:-1], refs[-1]
    n = mixed_ref.shape[1]
    me = lax.axis_index("wide")
    for mask, turn_ref in zip(masks, refs):
        for side in range(2):
            rows = rows_of(me ^ mask ^ (far * side), n)
            out_ref[rows, :] = quick(turn_ref[side], mixed_ref[rows, :])


def last_rows_kernel(masks, far, mixed_ref, *refs):
    turn_refs, (_, out_ref, block_ref, sem_ref) = refs[:-4], refs[-4:]
    n = mixed_ref.shape[1]
    me = lax.axis_index("wide")
    copies = []
    for mask, turn_ref in zip(masks, turn_refs):
        for side in range(2):
            rows = rows_of(me ^ mask ^ (far * side), n)
            place = len(copies)
            block_ref[place] = quick(turn_ref[side], mixed_ref[rows, :])
            copy = pltpu.make_async_copy(block_ref.at[place], out_ref.at[rows, :], sem_ref.at[place])
            copy.start()
            copies.append(copy)
    for copy in copies:
        copy.wait()


def call(kernel, out_shape, scratch_shapes, flops, *args, **more):
    return pl.pallas_call(
        kernel,
        out_shape=out_shape,
        scratch_shapes=scratch_shapes,
        compiler_params=pltpu.CompilerParams(vmem_limit_bytes=48 * 1024 * 1024),
        cost_estimate=pl.CostEstimate(flops=flops, bytes_accessed=2**20, transcendentals=0),
        **more,
    )(*args)


def swap(shard, mask):
    return lax.ppermute(shard, "wide", [(i, i ^ mask) for i in range(lax.axis_size("wide"))])


def after(value, gate):
    return lax.optimization_barrier((value, gate))[0]


def spread_first(own, early, both, far, gate):
    pieces = [(0, (both,))]
    if early:
        pieces.append((far // 2, early))
    bit = far // 4
    while bit:
        pieces += [
            (mask | bit, tuple(swap(after(held, gate), bit) for held in couple))
            for mask, couple in pieces
        ]
        bit //= 2
    return [mask for mask, _ in pieces], [held for _, couple in pieces for held in couple]


def spread_second(both, far, gate):
    pieces = [(0, both)]
    bit = far // 2
    while bit:
        pieces += [
            (mask | bit, swap(after(held, gate) if mask and bit == 1 else held, bit))
            for mask, held in pieces
        ]
        bit //= 2
    return pieces


def body(factor):
    far = lax.axis_size("wide") // 2
    me = lax.axis_index("wide")
    order_size, n = factor.shape

    def like(*shape):
        return jax.ShapeDtypeStruct(shape, jnp.float32)

    one, two, tall = like(1, n, n), like(2, n, n), like(order_size, n)
    own = lax.dynamic_slice_in_dim(factor, me * n, n, 0)
    cross = lax.dynamic_slice_in_dim(factor, (me ^ far) * n, n, 0)
    packed, qt, m = call(first_kernel, (like(n + n // 2, n), one, one), [], 2**32, own)
    packed = swap(packed, far)
    early = (swap(qt, far // 2), swap(qt, far // 2 | far)) if far > 1 else ()
    columns, right, moved = call(
        columns_kernel, (tall, like(order_size // 2, n), like(n, n)), [], 2**28, factor, cross, qt
    )
    right = swap(right, far)
    scratch = [pltpu.VMEM((2, n, n), jnp.float32)] * 2
    second, both = call(second_kernel, (two, two), scratch, 2**34, packed, m, qt, moved)
    masks, firsts = spread_first(qt, early, both, far, second)
    turned, turn, eigen_basis = call(
        functools.partial(turn_kernel, far),
        (tall, like(n, n), tall),
        [],
        2**31,
        columns,
        second,
        both,
    )
    mixed = call(
        functools.partial(trade_kernel, masks, far),
        tall,
        [pltpu.VMEM((order_size, n), jnp.float32)],
        2**31,
        turned,
        turn,
        right,
        *firsts,
    )
    pieces = spread_second(second, far, mixed)
    soon = [piece for piece in pieces if piece[0] < 2 or not piece[0] & 1]
    late = [piece for piece in pieces if piece[0] >= 2 and piece[0] & 1]
    masks, held = zip(*soon)
    rotated = call(functools.partial(rows_kernel, masks, far), tall, [], 2**29, mixed, *held)
    if late:
        masks, held = zip(*late)
        anywhere = pl.BlockSpec(memory_space=pl.ANY)
        inside = pl.BlockSpec(memory_space=pltpu.VMEM)
        rotated = call(
            functools.partial(last_rows_kernel, masks, far),
            tall,
            [
                pltpu.VMEM((2 * len(late), n, n), jnp.float32),
                pltpu.SemaphoreType.DMA((2 * len(late),)),
            ],
            2**29,
            mixed,
            *held,
            rotated,
            in_specs=[inside] * (1 + len(late)) + [anywhere],
            out_specs=anywhere,
            input_output_aliases={1 + len(late): 0},
        )
    return (rotated, eigen_basis)


def solution(mesh):
    return jax.shard_map(
        body,
        mesh=mesh,
        in_specs=(P("layer", "wide"),),
        out_specs=(P("layer", "wide"), P("layer", "wide")),
        check_vma=False,
    )
```

```python
import functools
import jax
import jax.numpy as jnp
from jax import lax
from jax.experimental import pallas as pl
from jax.experimental.pallas import tpu as pltpu
from jax.sharding import PartitionSpec as P

SWEEPS = 3
FLOOR = 0.01
TOLERANCE = 3e-6


def schedule(bound, steps=None, weight=1.0, goal=1e-6):
    theta = bound / (2.0 + bound)
    mus = []
    while len(mus) < steps if steps else theta > goal:
        mus.append(2.0 / (2.0 - theta * theta))
        theta = theta * theta / (2.0 - theta * theta)
    return 1.0 / (1.0 + 0.5 * bound), tuple(mus), weight


def split(x):
    high = x.astype(jnp.bfloat16)
    x = x - high.astype(jnp.float32)
    middle = x.astype(jnp.bfloat16)
    return high, middle, (x - middle.astype(jnp.float32)).astype(jnp.bfloat16)


def below(*parts):
    return tuple(jnp.concatenate(each, axis=0) for each in zip(*parts))


def product(a, b):
    a_high, a_middle, a_low = a
    b_high, b_middle, b_low = b
    n = b_high.shape[1]
    wide = jnp.concatenate([b_high, b_middle], axis=1)
    most = jnp.dot(
        jnp.concatenate([a_high, a_middle], axis=1),
        jnp.concatenate([wide, wide], axis=0),
        preferred_element_type=jnp.float32,
    )
    rest = jnp.dot(
        jnp.concatenate([a_high, a_low], axis=1),
        jnp.concatenate([b_low, b_high], axis=0),
        preferred_element_type=jnp.float32,
    )
    return most[:, :n] + (most[:, n:] + rest)


def exact(a, b):
    return jnp.dot(a, b, precision=lax.Precision.HIGHEST, preferred_element_type=jnp.float32)


def identity_of(n):
    row = lax.broadcasted_iota(jnp.int32, (n, n), 0)
    col = lax.broadcasted_iota(jnp.int32, (n, n), 1)
    return (row == col).astype(jnp.float32)


def ratios_of(m, eye):
    kept = m * eye
    spread = jnp.sum(kept, axis=0, keepdims=True) - jnp.sum(kept, axis=1, keepdims=True)
    return m * spread / (spread * spread + 2.0 * m * m + FLOOR)


def sure_sweep(m, qt, eye):
    n = m.shape[0]
    ratios = ratios_of(m, eye)
    a = 0.25 * (ratios - ratios.T)
    system = eye - exact(a, a)
    scale, mus, _ = schedule(n * n / 32.0)

    def newton(_, y):
        return y + exact(y, eye - exact(system, y))

    y = lax.fori_loop(0, len(mus) + 6, newton, scale * eye)
    x = exact(y, eye + a)
    x = x + exact(x, eye - (x - exact(a, x)))
    turn = 2.0 * x - eye
    return exact(turn.T, exact(m, turn)), exact(turn.T, qt)


def solve(blocks, plans, eye, keep):
    n = eye.shape[0]
    some = range(len(blocks))
    ms, qts = list(blocks), None
    worst = jnp.zeros((1, n), jnp.float32)
    for index, (scale, mus, weight) in enumerate(plans):
        carried = keep or index + 1 < len(plans)
        skews = [0.5 * ratios_of(m, eye) for m in ms]
        parts = [split(a) for a in skews]
        if carried:
            firsts = [product(below(a, split(m)), a) for a, m in zip(parts, ms)]
        else:
            firsts = [product(a, a) for a in parts]
        errors = [(1.0 - scale) * eye + scale * first[:n] for first in firsts]
        stacks = [scale * (eye - a) for a in skews]
        if carried:
            stacks = [
                jnp.concatenate([stack, scale * (m + first[n:])], axis=0)
                for stack, m, first in zip(stacks, ms, firsts)
            ]
        for mu in mus:
            parts = [split(error) for error in errors]
            if len(parts) == 1:
                squares = [product(part, part) for part in parts]
                steps = [product(split(stack), part) for part, stack in zip(parts, stacks)]
            else:
                both = [product(below(part, split(stack)), part) for part, stack in zip(parts, stacks)]
                squares, steps = [each[:n] for each in both], [each[n:] for each in both]
            errors = [(1.0 - mu) * eye + mu * square for square in squares]
            stacks = [mu * (stack + step) for stack, step in zip(stacks, steps)]
        for error in errors:
            worst = worst + weight * jnp.sum(error * error, axis=0, keepdims=True)
        backs = [2.0 * stack[:n] - eye for stack in stacks]
        rights = [[] for _ in some]
        if carried:
            rights = [[2.0 * stack[n:] - m] for stack, m in zip(stacks, ms)]
        if qts is not None:
            rights = [right + [qt] for right, qt in zip(rights, qts)]
        turned = [
            product(split(back), split(jnp.concatenate(right, axis=1)))
            for back, right in zip(backs, rights)
        ]
        qts = backs if qts is None else [both[:, -n:] for both in turned]
        if carried:
            ms = [both[:, :n] for both in turned]
    return ms, qts, worst


def settled(worst):
    return jnp.sum(worst) <= TOLERANCE * TOLERANCE * worst.shape[1]


def solve_surely(blocks, m_ref, qt_ref, eye):
    for k in range(len(blocks)):
        m_ref[k] = blocks[k]
        qt_ref[k] = eye

    def again(step, carry):
        k = step // SWEEPS
        m_ref[k], qt_ref[k] = sure_sweep(m_ref[k], qt_ref[k], eye)
        return carry

    lax.fori_loop(0, SWEEPS * len(blocks), again, 0)


PLANS = (
    (schedule(4.0, 4), schedule(3.0, 4), schedule(0.95, 3)),
    (schedule(0.8, 3), schedule(0.5, 3), schedule(0.2, 2, 0.01)),
)


def halves(x):
    high = x.astype(jnp.bfloat16)
    return high, (x - high.astype(jnp.float32)).astype(jnp.bfloat16)


def quick(a, b):
    n = b.shape[1]
    wide = jnp.concatenate(halves(b), axis=1)
    both = jnp.dot(
        jnp.concatenate(halves(a), axis=1),
        jnp.concatenate([wide, wide], axis=0),
        preferred_element_type=jnp.float32,
    )
    return both[:, :n] + both[:, n:]


def pair_up(first, last, corner):
    n = first.shape[0]
    row = lax.broadcasted_iota(jnp.int32, (n, n), 0) < n // 2
    col = lax.broadcasted_iota(jnp.int32, (n, n), 1) < n // 2
    return jnp.where(row == col, jnp.where(row, first, last), corner + corner.T)


def rows_of(pair, n):
    return pl.ds(pl.multiple_of(pair * n, n), n)


def first_kernel(own_ref, packed_ref, qt_ref, m_ref):
    n = own_ref.shape[0]
    half = n // 2
    eye = identity_of(n)
    col = lax.broadcasted_iota(jnp.int32, (half, n), 1) < half

    def finish(m, qt):
        packed_ref[:n, :] = qt
        packed_ref[n:, :] = jnp.where(col, m[:half], m[half:])

    (m,), (qt,), worst = solve([own_ref[...]], PLANS[0], eye, True)
    qt_ref[0] = qt
    m_ref[0] = m
    finish(m, qt)

    @pl.when(jnp.logical_not(settled(worst)))
    def _():
        solve_surely([own_ref[...]], m_ref, qt_ref, eye)
        finish(m_ref[0], qt_ref[0])


def columns_kernel(factor_ref, cross_ref, qt_ref, columns_ref, right_ref, moved_ref):
    order_size, n = factor_ref.shape
    half, middle = n // 2, order_size // 2
    turn = qt_ref[0].T
    moved_ref[...] = product(split(cross_ref[...]), split(turn))
    for start in range(0, middle, n):
        upper = quick(factor_ref[start : start + n, :], turn)
        lower = quick(factor_ref[middle + start : middle + start + n, :], turn)
        columns_ref[start : start + n, :] = upper
        columns_ref[middle + start : middle + start + n, :] = lower
        right_ref[start : start + n, :] = jnp.concatenate([upper[:, half:], lower[:, half:]], axis=1)


def second_kernel(packed_ref, m_in_ref, own_ref, moved_ref, second_ref, first_ref, block_ref, m_ref):
    n = moved_ref.shape[0]
    eye = identity_of(n)
    qt, packed = packed_ref[:n, :], packed_ref[n:, :]
    first_ref[0] = own_ref[0]
    first_ref[1] = qt
    cross = product(split(qt), split(moved_ref[...]))
    own, partner = m_in_ref[0], jnp.concatenate([packed, packed], axis=0)
    row = lax.broadcasted_iota(jnp.int32, (n, n), 0) < n // 2
    col = lax.broadcasted_iota(jnp.int32, (n, n), 1) < n // 2
    lower = jnp.where(jnp.logical_and(jnp.logical_not(row), col), cross, 0.0)
    upper = jnp.where(jnp.logical_and(row, jnp.logical_not(col)), cross, 0.0)
    blocks = [pair_up(own, partner, lower), pair_up(partner, own, upper)]
    block_ref[0], block_ref[1] = blocks
    _, (second_ref[0], second_ref[1]), worst = solve(blocks, PLANS[1], eye, False)

    @pl.when(jnp.logical_not(settled(worst)))
    def _():
        solve_surely([block_ref[0], block_ref[1]], m_ref, second_ref, eye)


def turn_kernel(far, columns_ref, second_ref, first_ref, turned_ref, turn_ref, out_ref):
    order_size, n = columns_ref.shape
    half = n // 2
    me = lax.axis_index("wide")
    row = lax.broadcasted_iota(jnp.int32, (n, n), 0) < half
    turn = second_ref[0].T
    turn_ref[...] = turn
    out_ref[...] = jnp.zeros_like(out_ref)
    out_ref[rows_of(me, n), :] = quick(jnp.where(row, first_ref[0], 0.0).T, turn)
    out_ref[rows_of(me ^ far, n), :] = quick(jnp.where(row, 0.0, first_ref[1]).T, turn)
    upper = jnp.where(row, turn, 0.0)
    for start in range(0, order_size, n):
        turned_ref[start : start + n, :] = quick(columns_ref[start : start + n, :], upper)


def trade_kernel(masks, far, turned_ref, turn_ref, right_ref, *refs):
    refs, mixed_ref, whole_ref = refs[:-2], refs[-2], refs[-1]
    order_size, n = turned_ref.shape
    half, middle = n // 2, order_size // 2
    me = lax.axis_index("wide")
    row = lax.broadcasted_iota(jnp.int32, (n, n), 0) < half
    turn = turn_ref[...]
    first = jnp.where(row, jnp.concatenate([turn[half:], turn[half:]], axis=0), 0.0)
    last = jnp.where(row, 0.0, turn)
    for start in range(0, middle, n):
        upper, lower = slice(start, start + n), slice(middle + start, middle + start + n)
        whole_ref[upper, :] = turned_ref[upper, :] + quick(right_ref[upper, :], first)
        whole_ref[lower, :] = turned_ref[lower, :] + quick(right_ref[upper, :], last)
    for mask, (near_ref, away_ref) in zip(masks, two_by_two(refs)):
        pair, other = rows_of(me ^ mask, n), rows_of(me ^ mask ^ far, n)
        near = quick(near_ref[...], whole_ref[pair, :])
        away = quick(away_ref[...], whole_ref[other, :])
        mixed_ref[pair, :] = jnp.concatenate([near[:half], away[half:]], axis=0)
        mixed_ref[other, :] = jnp.concatenate([away[:half], near[half:]], axis=0)


def two_by_two(refs):
    couples, held = [], []
    for ref in refs:
        held += [ref.at[side] for side in range(ref.shape[0])]
        if len(held) == 2:
            couples.append(held)
            held = []
    return couples


def rows_kernel(masks, far, mixed_ref, *refs):
    refs, out_ref = refs[:-1], refs[-1]
    n = mixed_ref.shape[1]
    me = lax.axis_index("wide")
    for mask, turn_ref in zip(masks, refs):
        for side in range(2):
            rows = rows_of(me ^ mask ^ (far * side), n)
            out_ref[rows, :] = quick(turn_ref[side], mixed_ref[rows, :])


def last_rows_kernel(masks, far, mixed_ref, *refs):
    turn_refs, (_, out_ref, block_ref, sem_ref) = refs[:-4], refs[-4:]
    n = mixed_ref.shape[1]
    me = lax.axis_index("wide")
    copies = []
    for mask, turn_ref in zip(masks, turn_refs):
        for side in range(2):
            rows = rows_of(me ^ mask ^ (far * side), n)
            place = len(copies)
            block_ref[place] = quick(turn_ref[side], mixed_ref[rows, :])
            copy = pltpu.make_async_copy(block_ref.at[place], out_ref.at[rows, :], sem_ref.at[place])
            copy.start()
            copies.append(copy)
    for copy in copies:
        copy.wait()


def call(kernel, out_shape, scratch_shapes, flops, *args, **more):
    return pl.pallas_call(
        kernel,
        out_shape=out_shape,
        scratch_shapes=scratch_shapes,
        compiler_params=pltpu.CompilerParams(vmem_limit_bytes=48 * 1024 * 1024),
        cost_estimate=pl.CostEstimate(flops=flops, bytes_accessed=2**20, transcendentals=0),
        **more,
    )(*args)


def swap(shard, mask):
    return lax.ppermute(shard, "wide", [(i, i ^ mask) for i in range(lax.axis_size("wide"))])


def after(value, gate):
    return lax.optimization_barrier((value, gate))[0]


def spread_first(own, early, both, far, gate):
    pieces = [(0, (both,))]
    if early:
        pieces.append((far // 2, early))
    bit = far // 4
    while bit:
        pieces += [
            (mask | bit, tuple(swap(after(held, gate), bit) for held in couple))
            for mask, couple in pieces
        ]
        bit //= 2
    return [mask for mask, _ in pieces], [held for _, couple in pieces for held in couple]


def spread_second(both, far, gate):
    pieces = [(0, both)]
    bit = far // 2
    while bit:
        pieces += [
            (mask | bit, swap(after(held, gate) if mask and bit == 1 else held, bit))
            for mask, held in pieces
        ]
        bit //= 2
    return pieces


def body(factor):
    far = lax.axis_size("wide") // 2
    me = lax.axis_index("wide")
    order_size, n = factor.shape

    def like(*shape):
        return jax.ShapeDtypeStruct(shape, jnp.float32)

    one, two, tall = like(1, n, n), like(2, n, n), like(order_size, n)
    own = lax.dynamic_slice_in_dim(factor, me * n, n, 0)
    cross = lax.dynamic_slice_in_dim(factor, (me ^ far) * n, n, 0)
    packed, qt, m = call(first_kernel, (like(n + n // 2, n), one, one), [], 2**32, own)
    packed = swap(packed, far)
    early = (swap(qt, far // 2), swap(qt, far // 2 | far)) if far > 1 else ()
    columns, right, moved = call(
        columns_kernel, (tall, like(order_size // 2, n), like(n, n)), [], 2**28, factor, cross, qt
    )
    right = swap(right, far)
    scratch = [pltpu.VMEM((2, n, n), jnp.float32)] * 2
    second, both = call(second_kernel, (two, two), scratch, 2**34, packed, m, qt, moved)
    masks, firsts = spread_first(qt, early, both, far, second)
    turned, turn, eigen_basis = call(
        functools.partial(turn_kernel, far),
        (tall, like(n, n), tall),
        [],
        2**31,
        columns,
        second,
        both,
    )
    mixed = call(
        functools.partial(trade_kernel, masks, far),
        tall,
        [pltpu.VMEM((order_size, n), jnp.float32)],
        2**31,
        turned,
        turn,
        right,
        *firsts,
    )
    pieces = spread_second(second, far, mixed)
    soon = [piece for piece in pieces if piece[0] < 2 or not piece[0] & 1]
    late = [piece for piece in pieces if piece[0] >= 2 and piece[0] & 1]
    masks, held = zip(*soon)
    rotated = call(functools.partial(rows_kernel, masks, far), tall, [], 2**29, mixed, *held)
    if late:
        masks, held = zip(*late)
        anywhere = pl.BlockSpec(memory_space=pl.ANY)
        inside = pl.BlockSpec(memory_space=pltpu.VMEM)
        rotated = call(
            functools.partial(last_rows_kernel, masks, far),
            tall,
            [
                pltpu.VMEM((2 * len(late), n, n), jnp.float32),
                pltpu.SemaphoreType.DMA((2 * len(late),)),
            ],
            2**29,
            mixed,
            *held,
            rotated,
            in_specs=[inside] * (1 + len(late)) + [anywhere],
            out_specs=anywhere,
            input_output_aliases={1 + len(late): 0},
        )
    return (rotated, eigen_basis)


def solution(mesh):
    return jax.shard_map(
        body,
        mesh=mesh,
        in_specs=(P("layer", "wide"),),
        out_specs=(P("layer", "wide"), P("layer", "wide")),
        check_vma=False,
    )
```

```python
import functools
import jax
import jax.numpy as jnp
from jax import lax
from jax.experimental import pallas as pl
from jax.experimental.pallas import tpu as pltpu
from jax.sharding import PartitionSpec as P

SWEEPS = 3
FLOOR = 0.01
TOLERANCE = 3e-6


def schedule(bound, steps=None, weight=1.0, goal=1e-6):
    theta = bound / (2.0 + bound)
    mus = []
    while len(mus) < steps if steps else theta > goal:
        mus.append(2.0 / (2.0 - theta * theta))
        theta = theta * theta / (2.0 - theta * theta)
    return 1.0 / (1.0 + 0.5 * bound), tuple(mus), weight


def split(x):
    high = x.astype(jnp.bfloat16)
    x = x - high.astype(jnp.float32)
    middle = x.astype(jnp.bfloat16)
    return high, middle, (x - middle.astype(jnp.float32)).astype(jnp.bfloat16)


def below(*parts):
    return tuple(jnp.concatenate(each, axis=0) for each in zip(*parts))


def product(a, b):
    a_high, a_middle, a_low = a
    b_high, b_middle, b_low = b
    n = b_high.shape[1]
    wide = jnp.concatenate([b_high, b_middle], axis=1)
    most = jnp.dot(
        jnp.concatenate([a_high, a_middle], axis=1),
        jnp.concatenate([wide, wide], axis=0),
        preferred_element_type=jnp.float32,
    )
    rest = jnp.dot(
        jnp.concatenate([a_high, a_low], axis=1),
        jnp.concatenate([b_low, b_high], axis=0),
        preferred_element_type=jnp.float32,
    )
    return most[:, :n] + (most[:, n:] + rest)


def exact(a, b):
    return jnp.dot(a, b, precision=lax.Precision.HIGHEST, preferred_element_type=jnp.float32)


def identity_of(n):
    row = lax.broadcasted_iota(jnp.int32, (n, n), 0)
    col = lax.broadcasted_iota(jnp.int32, (n, n), 1)
    return (row == col).astype(jnp.float32)


def ratios_of(m, eye):
    kept = m * eye
    spread = jnp.sum(kept, axis=0, keepdims=True) - jnp.sum(kept, axis=1, keepdims=True)
    return m * spread / (spread * spread + 2.0 * m * m + FLOOR)


def sure_sweep(m, qt, eye):
    n = m.shape[0]
    ratios = ratios_of(m, eye)
    a = 0.25 * (ratios - ratios.T)
    system = eye - exact(a, a)
    scale, mus, _ = schedule(n * n / 32.0)

    def newton(_, y):
        return y + exact(y, eye - exact(system, y))

    y = lax.fori_loop(0, len(mus) + 6, newton, scale * eye)
    x = exact(y, eye + a)
    x = x + exact(x, eye - (x - exact(a, x)))
    turn = 2.0 * x - eye
    return exact(turn.T, exact(m, turn)), exact(turn.T, qt)


def solve(blocks, plans, eye, keep):
    n = eye.shape[0]
    some = range(len(blocks))
    ms, qts = list(blocks), None
    worst = jnp.zeros((1, n), jnp.float32)
    for index, (scale, mus, weight) in enumerate(plans):
        carried = keep or index + 1 < len(plans)
        skews = [0.5 * ratios_of(m, eye) for m in ms]
        parts = [split(a) for a in skews]
        if carried:
            firsts = [product(below(a, split(m)), a) for a, m in zip(parts, ms)]
        else:
            firsts = [product(a, a) for a in parts]
        errors = [(1.0 - scale) * eye + scale * first[:n] for first in firsts]
        stacks = [scale * (eye - a) for a in skews]
        if carried:
            stacks = [
                jnp.concatenate([stack, scale * (m + first[n:])], axis=0)
                for stack, m, first in zip(stacks, ms, firsts)
            ]
        for mu in mus:
            parts = [split(error) for error in errors]
            if len(parts) == 1:
                squares = [product(part, part) for part in parts]
                steps = [product(split(stack), part) for part, stack in zip(parts, stacks)]
            else:
                both = [product(below(part, split(stack)), part) for part, stack in zip(parts, stacks)]
                squares, steps = [each[:n] for each in both], [each[n:] for each in both]
            errors = [(1.0 - mu) * eye + mu * square for square in squares]
            stacks = [mu * (stack + step) for stack, step in zip(stacks, steps)]
        for error in errors:
            worst = worst + weight * jnp.sum(error * error, axis=0, keepdims=True)
        backs = [2.0 * stack[:n] - eye for stack in stacks]
        rights = [[] for _ in some]
        if carried:
            rights = [[2.0 * stack[n:] - m] for stack, m in zip(stacks, ms)]
        if qts is not None:
            rights = [right + [qt] for right, qt in zip(rights, qts)]
        turned = [
            product(split(back), split(jnp.concatenate(right, axis=1)))
            for back, right in zip(backs, rights)
        ]
        qts = backs if qts is None else [both[:, -n:] for both in turned]
        if carried:
            ms = [both[:, :n] for both in turned]
    return ms, qts, worst


def settled(worst):
    return jnp.sum(worst) <= TOLERANCE * TOLERANCE * worst.shape[1]


def solve_surely(blocks, m_ref, qt_ref, eye):
    for k in range(len(blocks)):
        m_ref[k] = blocks[k]
        qt_ref[k] = eye

    def again(step, carry):
        k = step // SWEEPS
        m_ref[k], qt_ref[k] = sure_sweep(m_ref[k], qt_ref[k], eye)
        return carry

    lax.fori_loop(0, SWEEPS * len(blocks), again, 0)


PLANS = (
    (schedule(4.0, 4), schedule(3.0, 4), schedule(0.95, 3)),
    (schedule(0.8, 3), schedule(0.5, 3), schedule(0.2, 2, 0.01)),
)


def halves(x):
    high = x.astype(jnp.bfloat16)
    return high, (x - high.astype(jnp.float32)).astype(jnp.bfloat16)


def quick(a, b):
    n = b.shape[1]
    wide = jnp.concatenate(halves(b), axis=1)
    both = jnp.dot(
        jnp.concatenate(halves(a), axis=1),
        jnp.concatenate([wide, wide], axis=0),
        preferred_element_type=jnp.float32,
    )
    return both[:, :n] + both[:, n:]


def pair_up(first, last, corner):
    n = first.shape[0]
    row = lax.broadcasted_iota(jnp.int32, (n, n), 0) < n // 2
    col = lax.broadcasted_iota(jnp.int32, (n, n), 1) < n // 2
    return jnp.where(row == col, jnp.where(row, first, last), corner + corner.T)


def rows_of(pair, n):
    return pl.ds(pl.multiple_of(pair * n, n), n)


def first_kernel(own_ref, packed_ref, qt_ref, m_ref):
    n = own_ref.shape[0]
    half = n // 2
    eye = identity_of(n)
    col = lax.broadcasted_iota(jnp.int32, (half, n), 1) < half

    def finish(m, qt):
        packed_ref[:n, :] = qt
        packed_ref[n:, :] = jnp.where(col, m[:half], m[half:])

    (m,), (qt,), worst = solve([own_ref[...]], PLANS[0], eye, True)
    qt_ref[0] = qt
    m_ref[0] = m
    finish(m, qt)

    @pl.when(jnp.logical_not(settled(worst)))
    def _():
        solve_surely([own_ref[...]], m_ref, qt_ref, eye)
        finish(m_ref[0], qt_ref[0])


def columns_kernel(far, factor_ref, qt_ref, columns_ref, right_ref, moved_ref):
    order_size, n = factor_ref.shape
    half, middle = n // 2, order_size // 2
    turn = qt_ref[0].T
    moved_ref[...] = product(
        split(factor_ref[rows_of(lax.axis_index("wide") ^ far, n), :]), split(turn)
    )
    for start in range(0, middle, n):
        upper = quick(factor_ref[start : start + n, :], turn)
        lower = quick(factor_ref[middle + start : middle + start + n, :], turn)
        columns_ref[start : start + n, :] = upper
        columns_ref[middle + start : middle + start + n, :] = lower
        right_ref[start : start + n, :] = jnp.concatenate([upper[:, half:], lower[:, half:]], axis=1)


def second_kernel(packed_ref, m_in_ref, own_ref, moved_ref, second_ref, first_ref, block_ref, m_ref):
    n = moved_ref.shape[0]
    eye = identity_of(n)
    qt, packed = packed_ref[:n, :], packed_ref[n:, :]
    first_ref[0] = own_ref[0]
    first_ref[1] = qt
    cross = product(split(qt), split(moved_ref[...]))
    own, partner = m_in_ref[0], jnp.concatenate([packed, packed], axis=0)
    row = lax.broadcasted_iota(jnp.int32, (n, n), 0) < n // 2
    col = lax.broadcasted_iota(jnp.int32, (n, n), 1) < n // 2
    lower = jnp.where(jnp.logical_and(jnp.logical_not(row), col), cross, 0.0)
    upper = jnp.where(jnp.logical_and(row, jnp.logical_not(col)), cross, 0.0)
    blocks = [pair_up(own, partner, lower), pair_up(partner, own, upper)]
    block_ref[0], block_ref[1] = blocks
    _, (second_ref[0], second_ref[1]), worst = solve(blocks, PLANS[1], eye, False)

    @pl.when(jnp.logical_not(settled(worst)))
    def _():
        solve_surely([block_ref[0], block_ref[1]], m_ref, second_ref, eye)


def turn_kernel(far, columns_ref, second_ref, first_ref, turned_ref, turn_ref, out_ref):
    order_size, n = columns_ref.shape
    half = n // 2
    me = lax.axis_index("wide")
    row = lax.broadcasted_iota(jnp.int32, (n, n), 0) < half
    turn = second_ref[0].T
    turn_ref[...] = turn
    out_ref[...] = jnp.zeros_like(out_ref)
    out_ref[rows_of(me, n), :] = quick(jnp.where(row, first_ref[0], 0.0).T, turn)
    out_ref[rows_of(me ^ far, n), :] = quick(jnp.where(row, 0.0, first_ref[1]).T, turn)
    upper = jnp.where(row, turn, 0.0)
    for start in range(0, order_size, n):
        turned_ref[start : start + n, :] = quick(columns_ref[start : start + n, :], upper)


def trade_kernel(masks, far, turned_ref, turn_ref, right_ref, *refs):
    refs, mixed_ref, whole_ref = refs[:-2], refs[-2], refs[-1]
    order_size, n = turned_ref.shape
    half, middle = n // 2, order_size // 2
    me = lax.axis_index("wide")
    row = lax.broadcasted_iota(jnp.int32, (n, n), 0) < half
    turn = turn_ref[...]
    first = jnp.where(row, jnp.concatenate([turn[half:], turn[half:]], axis=0), 0.0)
    last = jnp.where(row, 0.0, turn)
    for start in range(0, middle, n):
        upper, lower = slice(start, start + n), slice(middle + start, middle + start + n)
        whole_ref[upper, :] = turned_ref[upper, :] + quick(right_ref[upper, :], first)
        whole_ref[lower, :] = turned_ref[lower, :] + quick(right_ref[upper, :], last)
    for mask, (near_ref, away_ref) in zip(masks, two_by_two(refs)):
        pair, other = rows_of(me ^ mask, n), rows_of(me ^ mask ^ far, n)
        near = quick(near_ref[...], whole_ref[pair, :])
        away = quick(away_ref[...], whole_ref[other, :])
        mixed_ref[pair, :] = jnp.concatenate([near[:half], away[half:]], axis=0)
        mixed_ref[other, :] = jnp.concatenate([away[:half], near[half:]], axis=0)


def two_by_two(refs):
    couples, held = [], []
    for ref in refs:
        held += [ref.at[side] for side in range(ref.shape[0])]
        if len(held) == 2:
            couples.append(held)
            held = []
    return couples


def rows_kernel(masks, far, mixed_ref, *refs):
    turn_refs, (out_ref, block_ref, sem_ref) = refs[: len(masks)], refs[-3:]
    n = mixed_ref.shape[1]
    me = lax.axis_index("wide")
    copies = []
    for mask, turn_ref in zip(masks, turn_refs):
        for side in range(2):
            rows = rows_of(me ^ mask ^ (far * side), n)
            place = len(copies)
            block_ref[place] = quick(turn_ref[side], mixed_ref[rows, :])
            copy = pltpu.make_async_copy(block_ref.at[place], out_ref.at[rows, :], sem_ref.at[place])
            copy.start()
            copies.append(copy)
    for copy in copies:
        copy.wait()


def call(kernel, out_shape, scratch_shapes, flops, *args, **more):
    return pl.pallas_call(
        kernel,
        out_shape=out_shape,
        scratch_shapes=scratch_shapes,
        compiler_params=pltpu.CompilerParams(vmem_limit_bytes=48 * 1024 * 1024),
        cost_estimate=pl.CostEstimate(flops=flops, bytes_accessed=2**20, transcendentals=0),
        **more,
    )(*args)


def swap(shard, mask):
    return lax.ppermute(shard, "wide", [(i, i ^ mask) for i in range(lax.axis_size("wide"))])


def after(value, gate):
    return lax.optimization_barrier((value, gate))[0]


def spread_first(own, early, both, far, gate):
    pieces = [(0, (both,))]
    if early:
        pieces.append((far // 2, early))
    bit = far // 4
    while bit:
        pieces += [
            (mask | bit, tuple(swap(after(held, gate), bit) for held in couple))
            for mask, couple in pieces
        ]
        bit //= 2
    return [mask for mask, _ in pieces], [held for _, couple in pieces for held in couple]


def spread_second(both, far, gate):
    pieces = [(0, both)]
    bit = far // 2
    while bit:
        pieces += [
            (mask | bit, swap(after(held, gate) if mask and bit == 1 else held, bit))
            for mask, held in pieces
        ]
        bit //= 2
    return pieces


def body(factor):
    far = lax.axis_size("wide") // 2
    me = lax.axis_index("wide")
    order_size, n = factor.shape

    def like(*shape):
        return jax.ShapeDtypeStruct(shape, jnp.float32)

    one, two, tall = like(1, n, n), like(2, n, n), like(order_size, n)
    own = lax.dynamic_slice_in_dim(factor, me * n, n, 0)
    packed, qt, m = call(first_kernel, (like(n + n // 2, n), one, one), [], 2**32, own)
    packed = swap(packed, far)
    early = (swap(qt, far // 2), swap(qt, far // 2 | far)) if far > 1 else ()
    columns, right, moved = call(
        functools.partial(columns_kernel, far), (tall, like(order_size // 2, n), like(n, n)), [], 2**28, factor, qt
    )
    right = swap(right, far)
    scratch = [pltpu.VMEM((2, n, n), jnp.float32)] * 2
    second, both = call(second_kernel, (two, two), scratch, 2**34, packed, m, qt, moved)
    masks, firsts = spread_first(qt, early, both, far, second)
    turned, turn, eigen_basis = call(
        functools.partial(turn_kernel, far),
        (tall, like(n, n), tall),
        [],
        2**31,
        columns,
        second,
        both,
    )
    mixed = call(
        functools.partial(trade_kernel, masks, far),
        tall,
        [pltpu.VMEM((order_size, n), jnp.float32)],
        2**31,
        turned,
        turn,
        right,
        *firsts,
    )
    pieces = spread_second(second, far, mixed)
    soon = [piece for piece in pieces if piece[0] < 2 or not piece[0] & 1]
    late = [piece for piece in pieces if piece[0] >= 2 and piece[0] & 1]
    rotated = ()
    for part in (soon, late):
        if part:
            masks, held = zip(*part)
            blocks = 2 * len(part)
            rotated = call(
                functools.partial(rows_kernel, masks, far),
                tall,
                [pltpu.VMEM((blocks, n, n), jnp.float32), pltpu.SemaphoreType.DMA((blocks,))],
                2**29,
                mixed,
                *held,
                *rotated,
                in_specs=[pl.BlockSpec(memory_space=pltpu.VMEM)] * (1 + len(part))
                + [pl.BlockSpec(memory_space=pl.ANY)] * len(rotated),
                out_specs=pl.BlockSpec(memory_space=pl.ANY),
                input_output_aliases={1 + len(part): 0} if rotated else {},
            )
            rotated = (rotated,)
    (rotated,) = rotated
    return (rotated, eigen_basis)


def solution(mesh):
    return jax.shard_map(
        body,
        mesh=mesh,
        in_specs=(P("layer", "wide"),),
        out_specs=(P("layer", "wide"), P("layer", "wide")),
        check_vma=False,
    )
```
